32 devices in a mesh: replica: 2 (over y), node: 4 (over z), local: 4 (over x, core).
Axes of the slice: x: 2, y: 2, z: 4, core: 2. Of those that a mesh axis runs over, the one named last changes fastest.
Arguments:
- tokens: bfloat16 [2048, 3584], P(('replica', 'node', 'local')), parts along dimension 0, may hold values from -6 to 6
- routes: int32 [2048, 8], P(('replica', 'node', 'local')), parts along dimension 0, may hold values from 0 to 7, as said below
- gates: float32 [2048, 8], P(('replica', 'node', 'local')), parts along dimension 0, may hold values from 0.05 to 0.6
- capacity: int32 [16], P('replica'), parts along dimension 0, may hold values from 6 to 8, as said below
- w_gate: bfloat16 [16, 3584, 512], P(('node', 'local')), may hold values from -0.09375 to 0.09375
- w_up: bfloat16 [16, 3584, 512], P(('node', 'local')), may hold values from -0.09375 to 0.09375
- w_down: bfloat16 [16, 512, 3584], P(('node', 'local')), may hold values from -0.1875 to 0.1875
Outputs:
- mixed: bfloat16 [2048, 3584], P(('replica', 'node', 'local')), parts along dimension 0
The draws below stay inside these ranges and needn't reach their ends.
There are 2 independent parts, one for each index of `replica`. The reference program is written for one: setup_inputs(seed, part) draws one part's arguments, and reference() takes and returns one part's arrays. A program takes and returns all parts, laid end to end along the dimension named above; an argument that names none is the same for every part. Nothing has to cross between parts.
Inputs may be any that keep to these rules, and one draw needn't show every extreme that they name: `routes`: each row names 8 different experts, all from at most 4 node groups; expert e lies in node group e // 2. Some expert has capacity 8 and is named by 8 or more of the 64 rows of every device.
All inputs are finite; a program needn't handle non-finite values.
Results may differ from the reference program's by a relative error of at most 0.0095.
Values may be sent and summed in bfloat16 or wider, within the bound.
A program may use at most 128 MiB of HBM per device.

```python
import math
import jax
import jax.numpy as jnp
from jax import lax

D = 3584
FF = 1024
SHARDS = 2
TOPK = 8
GROUPS_MAX = 4
CAP = 8
TOK_DEV = 64
EXP_GROUP = 2
EXPERTS = 8
TOKENS = 1024
N_NODE = 4


def hot_expert(key):
    return jax.random.randint(key, (), 0, EXPERTS)


def draw_routes(key, part):
    hot = hot_expert(key)
    key = jax.random.fold_in(key, 1)
    first_key, second_key = jax.random.split(key)
    rows = jnp.arange(TOKENS, dtype=jnp.int32)
    forced = (rows % TOK_DEV < CAP)[:, None]
    group_iota = jnp.arange(N_NODE, dtype=jnp.int32)[None, :]
    group_big = (1 << 16) * N_NODE
    group_score = jax.random.randint(first_key, (TOKENS, N_NODE), 0, 1 << 16) * N_NODE + group_iota
    group_score = group_score + jnp.where(forced & (group_iota == hot // EXP_GROUP), group_big, 0)
    unused, groups = lax.top_k(group_score, GROUPS_MAX)
    allowed = jnp.any(groups[:, :, None] == group_iota[:, None, :], axis=1)
    allowed_e = jnp.repeat(allowed, EXP_GROUP, axis=1)
    expert_iota = jnp.arange(EXPERTS, dtype=jnp.int32)[None, :]
    expert_big = (1 << 16) * EXPERTS
    expert_score = jax.random.randint(second_key, (TOKENS, EXPERTS), 0, 1 << 16) * EXPERTS + expert_iota
    expert_score = expert_score + jnp.where(forced & (expert_iota == hot), expert_big, 0)
    expert_score = expert_score - jnp.where(allowed_e, 0, 2 * expert_big)
    unused, chosen = lax.top_k(expert_score, TOPK)
    return chosen.astype(jnp.int32)


def draw_capacity(key, part):
    hot = hot_expert(key)
    key = jax.random.fold_in(key, 2)
    values = jax.random.randint(key, (EXPERTS,), CAP - 2, CAP + 1)
    values = jnp.where(jnp.arange(EXPERTS) == hot, CAP, values)
    return values.astype(jnp.int32)


def level_of(stream_key, shape, pieces, least, top_value):
    def one(axis_at, shards_of):
        steps = jax.random.uniform(jax.random.fold_in(jax.random.fold_in(stream_key, 6), axis_at), (shards_of,), jnp.float32, least / len(pieces), top_value / len(pieces))
        return jnp.repeat(jnp.exp(steps), shape[axis_at] // shards_of).reshape((-1,) + (1,) * (len(shape) - axis_at - 1))

    factor_of = one(*pieces[0])
    for cut in pieces[1:]:
        factor_of = factor_of * one(*cut)
    return factor_of


def gaussian(key, shape, spread, reach, cuts=(), kind=jnp.bfloat16):
    drawn = spread * jax.random.normal(key, shape, jnp.float32)
    if cuts:
        drawn = drawn * level_of(key, shape, cuts, -0.22, 0.18)
    return jnp.clip(drawn, -reach, reach).astype(kind)


def setup_inputs(seed: int = 0, part: int = 0) -> dict:
    seeds = jax.random.split(jax.random.key(seed), 8)
    part_splits = jax.random.split(jax.random.fold_in(seeds[7], part), 8)
    tokens = gaussian(part_splits[0], (TOKENS, D), 1.0, 6.0, ((0, 16),))
    routes = draw_routes(jax.random.fold_in(jax.random.fold_in(seeds[7], part), 71), part)
    gates = jnp.clip(jnp.exp(math.log(0.6) - 2.4849067 * jax.random.uniform(part_splits[2], (TOKENS, TOPK), jnp.float32) ** level_of(part_splits[2], (TOKENS, TOPK), ((0, 16),), -0.2, 0.2)), 0.05, 0.6)
    capacity = draw_capacity(jax.random.fold_in(jax.random.fold_in(seeds[7], part), 71), part)
    w_gate = gaussian(seeds[4], (EXPERTS * SHARDS, D, FF // SHARDS), D ** -0.5, 0.09375, ((0, 16),))
    w_up = gaussian(seeds[5], (EXPERTS * SHARDS, D, FF // SHARDS), D ** -0.5, 0.09375, ((0, 16),))
    w_down = gaussian(seeds[6], (EXPERTS * SHARDS, FF // SHARDS, D), FF ** -0.5, 0.1875, ((0, 16),))
    return {"tokens": tokens, "routes": routes, "gates": gates, "capacity": capacity, "w_gate": w_gate, "w_up": w_up, "w_down": w_down}


def reference(tokens, routes, gates, capacity, w_gate, w_up, w_down):
    tok_all = tokens.shape[0]
    blocks = tok_all // TOK_DEV
    iota_e = jnp.arange(EXPERTS, dtype=jnp.int32)
    match = routes[:, :, None] == iota_e[None, None, :]
    chosen = jnp.sum(match.astype(jnp.int32), axis=1)
    gate_te = jnp.sum(jnp.where(match, gates[:, :, None], jnp.float32(0.0)), axis=1)
    blocked = chosen.reshape(blocks, TOK_DEV, EXPERTS)
    rank = (jnp.cumsum(blocked, axis=1) - blocked).reshape(tok_all, EXPERTS)
    kept = (chosen > 0) & (rank < capacity[None, :])
    tok_ids = jnp.arange(tok_all, dtype=jnp.int32)
    slot = (tok_ids // TOK_DEV)[:, None] * CAP + rank
    expert_rows = jnp.where(kept, iota_e[None, :], EXPERTS).astype(jnp.int32)
    slot_cols = jnp.where(kept, slot, 0).astype(jnp.int32)
    table = jnp.full((EXPERTS, blocks * CAP), tok_all, jnp.int32)
    table = table.at[expert_rows, slot_cols].set(jnp.broadcast_to(tok_ids[:, None], kept.shape), mode="drop")
    padded = jnp.concatenate([tokens, jnp.zeros((1, tokens.shape[1]), jnp.bfloat16)], axis=0)
    gate_pad = jnp.concatenate([gate_te, jnp.zeros((1, EXPERTS), jnp.float32)], axis=0)
    total = jnp.zeros((tok_all, tokens.shape[1]), jnp.float32)
    for group in range(N_NODE):
        def expert_step(step, accum):
            expert = (group * EXP_GROUP + step).astype(jnp.int32)
            index = table[expert]
            rows = padded[index]
            summed = jnp.zeros((rows.shape[0], tokens.shape[1]), jnp.float32)
            for part in range(SHARDS):
                row = expert * SHARDS + part
                gated = jnp.dot(rows, w_gate[row], preferred_element_type=jnp.float32)
                upper = jnp.dot(rows, w_up[row], preferred_element_type=jnp.float32)
                act = (jax.nn.silu(gated) * upper).astype(jnp.bfloat16)
                summed = summed + jnp.dot(act, w_down[row], preferred_element_type=jnp.float32)
            piece = summed.astype(jnp.bfloat16)
            weight = gate_pad[index, expert]
            return accum.at[index].add(weight[:, None] * piece.astype(jnp.float32))
        accum = jnp.zeros((tok_all + 1, tokens.shape[1]), jnp.float32)
        accum = lax.fori_loop(0, EXP_GROUP, expert_step, accum)
        total = total + accum[:tok_all].astype(jnp.bfloat16).astype(jnp.float32)
    return total.astype(jnp.bfloat16)
```

```python
import functools

import jax
import jax.numpy as jnp
from jax import lax
from jax.experimental import pallas as pl
from jax.experimental.pallas import tpu as pltpu
from jax.sharding import PartitionSpec as P

SHARDS = 2
CAP = 8
LANES = 128
CHUNKS = 2
MESH = pl.DeviceIdType.MESH


def dense_kernel(
    nodes,
    tokens_ref, routes_ref, gates_ref, cap_ref, wg_hbm, wu_hbm, wd_hbm,
    out_ref,
    wg, wu, wd, tok, gath, rows, act,
    pair_out, pair_in, summed, x_out, x_in, total, z_out, z_in, fin, fin_in,
    load_sem, gs_sem, gr_sem, ps_sem, pr_sem, xs_sem, xr_sem, zs_sem, zr_sem, fs_sem, fr_sem,
):
    node = lax.axis_index("node")
    local = lax.axis_index("local")
    xi = local // SHARDS
    core = local % SHARDS
    width = wg.shape[0]
    half = width // 2
    hidden = wg.shape[1]
    cols = half // CHUNKS
    blocks = nodes * 2 * SHARDS

    core_peer = {"local": xi * SHARDS + 1 - core}
    x_peer = {"local": (1 - xi) * SHARDS + core}

    def z_peer(d):
        return {"node": (node + d) % nodes}

    def slot(n, x, c):
        return (n * 2 + x) * SHARDS + c

    def remote(src, dst, send, recv, peer):
        return pltpu.make_async_remote_copy(
            src_ref=src, dst_ref=dst, send_sem=send, recv_sem=recv,
            device_id=peer, device_id_type=MESH,
        )

    tok_load = pltpu.make_async_copy(tokens_ref.at[pl.ds(0, 2 * CAP)], tok, load_sem.at[0])
    tok_load.start()
    loads = [
        pltpu.make_async_copy(wg_hbm.at[0], wg, load_sem.at[1]),
        pltpu.make_async_copy(wu_hbm.at[0], wu, load_sem.at[2]),
        pltpu.make_async_copy(wd_hbm.at[0], wd, load_sem.at[3]),
    ]
    for load in loads:
        load.start()

    barrier = pltpu.get_barrier_semaphore()
    peers = [core_peer, x_peer] + [z_peer(d) for d in range(1, nodes)]
    for peer in peers:
        pl.semaphore_signal(barrier, inc=1, device_id=peer, device_id_type=MESH)

    lane = lax.broadcasted_iota(jnp.int32, (CAP, LANES), 1)
    row = lax.broadcasted_iota(jnp.int32, (CAP, LANES), 0)
    table = jnp.zeros((CAP, LANES), jnp.float32)
    limit = jnp.zeros((CAP, LANES), jnp.int32)
    for k in range(routes_ref.shape[1]):
        table = table + jnp.where(routes_ref[:, k : k + 1] == lane, gates_ref[:, k : k + 1], 0.0)
        limit = jnp.where(lane == k, cap_ref[k], limit)
    table = jnp.where(row < limit, table, 0.0)
    high = table.astype(jnp.bfloat16).astype(jnp.float32)
    low = table - high

    tok_load.wait()
    mine = tok[...].astype(jnp.float32)[:CAP]
    top = jnp.concatenate([mine[:, :half], high], axis=1)
    bottom = jnp.concatenate([mine[:, half:], low], axis=1)
    own = slot(node, xi, core)
    gath[own] = jnp.concatenate([top, bottom], axis=0).astype(jnp.bfloat16)

    pl.semaphore_wait(barrier, len(peers))

    started = []
    pending = {}

    def send(key, index, s, peer):
        copy = remote(gath.at[s], gath.at[s], gs_sem.at[index], gr_sem.at[index], peer)
        copy.start()
        started.append(copy)
        pending[key] = copy

    for d in range(1, nodes):
        send(("z", d), d - 1, own, z_peer(d))
    send(("x", 0), nodes - 1, own, x_peer)
    send(("c", 0, 0), 2 * nodes - 1, own, core_peer)
    for d in range(1, nodes):
        pending[("z", d)].wait_recv()
        s = slot((node + nodes - d) % nodes, xi, core)
        send(("x", d), nodes - 1 + d, s, x_peer)
        send(("c", 0, d), 2 * nodes - 1 + d, s, core_peer)
    for d in range(nodes):
        pending[("x", d)].wait_recv()
        s = slot((node + nodes - d) % nodes, 1 - xi, core)
        send(("c", 1, d), 3 * nodes - 1 + d, s, core_peer)
    for x in range(2):
        for d in range(nodes):
            pending[("c", x, d)].wait_recv()

    got = gath[...].astype(jnp.float32)
    count = blocks * CAP
    rows[:, :half] = got[:, :CAP, :half].reshape(count, half).astype(jnp.bfloat16)
    rows[:, half:] = got[:, CAP:, :half].reshape(count, half).astype(jnp.bfloat16)
    expert = node * 2 + xi
    pair = (got[:, :CAP, half:] + got[:, CAP:, half:]).reshape(count, LANES)
    lanes = lax.broadcasted_iota(jnp.int32, (count, LANES), 1)
    weight = jnp.sum(jnp.where(lanes == expert, pair, 0.0), axis=1, keepdims=True)

    loads[0].wait()
    loads[1].wait()
    step = 256
    for n in range(hidden // step):
        at = pl.ds(n * step, step)
        gated = jnp.dot(rows[...], wg[:, at], preferred_element_type=jnp.float32)
        upper = jnp.dot(rows[...], wu[:, at], preferred_element_type=jnp.float32)
        act[:, at] = (jax.nn.silu(gated) * upper * weight).astype(jnp.bfloat16)
    loads[2].wait()

    def down(c, k):
        at = pl.ds(pl.multiple_of(c * half + k * cols, LANES), cols)
        return jnp.dot(act[...], wd[:, at], preferred_element_type=jnp.float32)

    pair_copies, x_copies, z_copies = [], [], []
    for k in range(CHUNKS):
        pair_out[k] = down(1 - core, k).astype(jnp.bfloat16)
        copy = remote(pair_out.at[k], pair_in.at[k], ps_sem.at[k], pr_sem.at[k], core_peer)
        copy.start()
        pair_copies.append(copy)
    for k in range(CHUNKS):
        part = down(core, k)
        pair_copies[k].wait_recv()
        part = part + pair_in[k].astype(jnp.float32)
        summed[k] = part.reshape(nodes, 2, SHARDS * CAP, cols)
        x_out[k] = summed[k, :, 1 - xi].astype(jnp.bfloat16)
        copy = remote(x_out.at[k], x_in.at[k], xs_sem.at[k], xr_sem.at[k], x_peer)
        copy.start()
        x_copies.append(copy)
    for k in range(CHUNKS):
        x_copies[k].wait_recv()
        part = summed[k, :, xi] + x_in[k].astype(jnp.float32)
        total[k] = part
        z_out[k] = part.astype(jnp.bfloat16)
        for d in range(1, nodes):
            i = k * (nodes - 1) + d - 1
            copy = remote(
                z_out.at[k, (node + d) % nodes], z_in.at[k, d - 1], zs_sem.at[i], zr_sem.at[i], z_peer(d)
            )
            copy.start()
            z_copies.append(copy)
    fin_copies = []
    for k in range(CHUNKS):
        part = total[k, node]
        for d in range(1, nodes):
            z_copies[k * (nodes - 1) + d - 1].wait_recv()
            part = part + z_in[k, d - 1].astype(jnp.float32)
        fin[k, 0] = part[:CAP]
        fin[k, 1] = part[CAP:]
        copy = remote(fin.at[k, 1 - core], fin_in.at[k], fs_sem.at[k], fr_sem.at[k], core_peer)
        copy.start()
        fin_copies.append(copy)
    for k in range(CHUNKS):
        at = pl.ds(pl.multiple_of(core * half + k * cols, LANES), cols)
        out_ref[:, at] = fin[k, core]
    for k in range(CHUNKS):
        fin_copies[k].wait_recv()
        at = pl.ds(pl.multiple_of((1 - core) * half + k * cols, LANES), cols)
        out_ref[:, at] = fin_in[k]
    for copy in started + pair_copies + x_copies + z_copies + fin_copies:
        copy.wait_send()


def dense_device(tokens, routes, gates, capacity, w_gate, w_up, w_down):
    nodes = lax.axis_size("node")
    tok_count, width = tokens.shape
    hidden = w_gate.shape[2]
    half = width // 2
    cols = half // CHUNKS
    blocks = nodes * 2 * SHARDS
    count = blocks * CAP
    bf, f32 = jnp.bfloat16, jnp.float32
    vmem = pl.BlockSpec(memory_space=pltpu.VMEM)
    smem = pl.BlockSpec(memory_space=pltpu.SMEM)
    hbm = pl.BlockSpec(memory_space=pl.ANY)
    dma = pltpu.SemaphoreType.DMA
    pair_rows = SHARDS * CAP
    out = pl.pallas_call(
        functools.partial(dense_kernel, nodes),
        out_shape=jax.ShapeDtypeStruct((CAP, width), f32),
        in_specs=[hbm, vmem, vmem, smem, hbm, hbm, hbm],
        out_specs=vmem,
        scratch_shapes=[
            pltpu.VMEM((width, hidden), bf),
            pltpu.VMEM((width, hidden), bf),
            pltpu.VMEM((hidden, width), bf),
            pltpu.VMEM((2 * CAP, width), bf),
            pltpu.VMEM((blocks, 2 * CAP, half + LANES), bf),
            pltpu.VMEM((count, width), bf),
            pltpu.VMEM((count, hidden), bf),
            pltpu.VMEM((CHUNKS, count, cols), bf),
            pltpu.VMEM((CHUNKS, count, cols), bf),
            pltpu.VMEM((CHUNKS, nodes, 2, pair_rows, cols), f32),
            pltpu.VMEM((CHUNKS, nodes, pair_rows, cols), bf),
            pltpu.VMEM((CHUNKS, nodes, pair_rows, cols), bf),
            pltpu.VMEM((CHUNKS, nodes, pair_rows, cols), f32),
            pltpu.VMEM((CHUNKS, nodes, pair_rows, cols), bf),
            pltpu.VMEM((CHUNKS, nodes - 1, pair_rows, cols), bf),
            pltpu.VMEM((CHUNKS, 2, CAP, cols), f32),
            pltpu.VMEM((CHUNKS, CAP, cols), f32),
            dma((4,)),
            dma((4 * nodes - 1,)),
            dma((4 * nodes - 1,)),
            dma((CHUNKS,)),
            dma((CHUNKS,)),
            dma((CHUNKS,)),
            dma((CHUNKS,)),
            dma((CHUNKS * (nodes - 1),)),
            dma((CHUNKS * (nodes - 1),)),
            dma((CHUNKS,)),
            dma((CHUNKS,)),
        ],
        compiler_params=pltpu.CompilerParams(
            collective_id=0, has_side_effects=True, vmem_limit_bytes=44 * 2**20
        ),
        cost_estimate=pl.CostEstimate(
            flops=6 * count * width * hidden, bytes_accessed=6 * width * hidden, transcendentals=count * hidden
        ),
    )(tokens, routes[:CAP], gates[:CAP], capacity, w_gate, w_up, w_down)
    return jnp.pad(out.astype(bf), ((0, tok_count - CAP), (0, 0)))


def per_device(tokens, routes, gates, capacity, w_gate, w_up, w_down):
    nodes = lax.axis_size("node")
    members = lax.axis_size("local")
    group_size = members // SHARDS
    experts = nodes * group_size
    tok_count, width = tokens.shape
    if experts == routes.shape[1] and group_size == 2 and members == 2 * SHARDS:
        return dense_device(tokens, routes, gates, capacity, w_gate, w_up, w_down)
    iota_e = jnp.arange(experts, dtype=jnp.int32)
    match = routes[:, :, None] == iota_e[None, None, :]
    chosen = jnp.sum(match.astype(jnp.int32), axis=1)
    gate_te = jnp.sum(jnp.where(match, gates[:, :, None], jnp.float32(0.0)), axis=1)
    rank = jnp.cumsum(chosen, axis=0) - chosen
    kept = (chosen > 0) & (rank < capacity[None, :])
    iota_c = jnp.arange(CAP, dtype=jnp.int32)
    place = (rank.T[:, None, :] == iota_c[None, :, None]) & kept.T[:, None, :]
    weighted = jnp.where(place, gate_te.T[:, None, :], jnp.float32(0.0))
    weighted = weighted.reshape(nodes, group_size, CAP, tok_count)
    gate_mat = w_gate[0]
    up_mat = w_up[0]
    down_mat = w_down[0]

    def read_back(back):
        back = back.reshape(nodes, group_size, SHARDS, CAP, width)
        return jnp.sum(back, axis=2).astype(jnp.bfloat16)

    place_bf = place.astype(jnp.bfloat16)
    slotted = jnp.einsum(
        "ect,td->ecd", place_bf, tokens, preferred_element_type=jnp.float32
    ).astype(jnp.bfloat16)
    slotted = slotted.reshape(nodes, group_size, CAP, width)
    wide = jnp.broadcast_to(slotted[:, :, None], (nodes, group_size, SHARDS, CAP, width))
    spread = wide.reshape(nodes, members, CAP, width)
    outgoing = spread.reshape(nodes * members, -1, width)
    arrived = lax.all_to_all(outgoing, ("node", "local"), split_axis=0, concat_axis=0, tiled=True)
    rows = arrived.reshape(-1, width)
    gated = jnp.dot(rows, gate_mat, preferred_element_type=jnp.float32)
    upper = jnp.dot(rows, up_mat, preferred_element_type=jnp.float32)
    act = (jax.nn.silu(gated) * upper).astype(jnp.bfloat16)
    back = lax.all_to_all(
        jnp.dot(act, down_mat, preferred_element_type=jnp.float32).reshape(arrived.shape),
        ("node", "local"),
        split_axis=0,
        concat_axis=0,
        tiled=True,
    )
    slot_gate = jnp.sum(weighted, axis=3)
    scaled = read_back(back).astype(jnp.float32) * slot_gate[:, :, :, None]
    high = scaled.astype(jnp.bfloat16)
    low = (scaled - high.astype(jnp.float32)).astype(jnp.bfloat16)
    pick = (weighted > 0.0).astype(jnp.bfloat16)
    summed = jnp.einsum("nmct,nmcd->ntd", pick, high, preferred_element_type=jnp.float32)
    summed = summed + jnp.einsum("nmct,nmcd->ntd", pick, low, preferred_element_type=jnp.float32)
    parts = summed.astype(jnp.bfloat16)
    return jnp.sum(parts.astype(jnp.float32), axis=0).astype(jnp.bfloat16)


def solution(mesh):
    return jax.shard_map(
        per_device,
        mesh=mesh,
        in_specs=(
            P(("replica", "node", "local"), None),
            P(("replica", "node", "local"), None),
            P(("replica", "node", "local"), None),
            P("replica"),
            P(("node", "local"), None, None),
            P(("node", "local"), None, None),
            P(("node", "local"), None, None),
        ),
        out_specs=P(("replica", "node", "local"), None),
        check_vma=False,
    )
```

```python
import functools

import jax
import jax.numpy as jnp
from jax import lax
from jax.experimental import pallas as pl
from jax.experimental.pallas import tpu as pltpu
from jax.sharding import PartitionSpec as P

SHARDS = 2
CAP = 8
LANES = 128
CHUNKS = 7
MESH = pl.DeviceIdType.MESH


def dense_kernel(
    nodes,
    tokens_hbm, routes_hbm, gates_hbm, cap_hbm, wg_hbm, wu_hbm, wd_hbm,
    out_ref,
    wg, wu, wd, tok, routes_t, gates_t, caps, gath, rows, act,
    pair_out, pair_in, summed, x_out, x_in, total, z_out, z_in, fin, fin_in,
    load_sem, gs_sem, gr_sem, ps_sem, pr_sem, xs_sem, xr_sem, zs_sem, zr_sem, fs_sem, fr_sem,
):
    node = lax.axis_index("node")
    local = lax.axis_index("local")
    xi = local // SHARDS
    core = local % SHARDS
    width = wg.shape[0]
    half = width // 2
    hidden = wg.shape[1]
    cols = half // CHUNKS
    blocks = nodes * 2 * SHARDS

    core_peer = {"local": xi * SHARDS + 1 - core}
    x_peer = {"local": (1 - xi) * SHARDS + core}

    def z_peer(d):
        return {"node": (node + d) % nodes}

    def slot(n, x, c):
        return (n * 2 + x) * SHARDS + c

    def remote(src, dst, send, recv, peer):
        return pltpu.make_async_remote_copy(
            src_ref=src, dst_ref=dst, send_sem=send, recv_sem=recv,
            device_id=peer, device_id_type=MESH,
        )

    small = [
        pltpu.make_async_copy(tokens_hbm.at[pl.ds(0, 2 * CAP)], tok, load_sem.at[0]),
        pltpu.make_async_copy(routes_hbm, routes_t, load_sem.at[4]),
        pltpu.make_async_copy(gates_hbm, gates_t, load_sem.at[5]),
        pltpu.make_async_copy(cap_hbm, caps, load_sem.at[6]),
    ]
    for load in small:
        load.start()
    loads = [
        pltpu.make_async_copy(wg_hbm.at[0], wg, load_sem.at[1]),
        pltpu.make_async_copy(wu_hbm.at[0], wu, load_sem.at[2]),
        pltpu.make_async_copy(wd_hbm.at[0], wd, load_sem.at[3]),
    ]
    for load in loads:
        load.start()

    barrier = pltpu.get_barrier_semaphore()
    peers = [core_peer, x_peer] + [z_peer(d) for d in range(1, nodes)]
    for peer in peers:
        pl.semaphore_signal(barrier, inc=1, device_id=peer, device_id_type=MESH)

    for load in small:
        load.wait()
    lane = lax.broadcasted_iota(jnp.int32, (CAP, LANES), 1)
    expert_of = lax.broadcasted_iota(jnp.int32, (CAP, LANES), 0)
    pad = jnp.zeros((routes_t.shape[0], LANES - routes_t.shape[1]))
    ids = jnp.concatenate([routes_t[...], pad.astype(jnp.int32)], axis=1)
    gate = jnp.concatenate([gates_t[...], pad.astype(jnp.float32)], axis=1)
    table = jnp.zeros((CAP, LANES), jnp.float32)
    limit = jnp.zeros((CAP, LANES), jnp.int32)
    for k in range(routes_t.shape[0]):
        table = table + jnp.where(ids[k : k + 1] == expert_of, gate[k : k + 1], 0.0)
        limit = jnp.where(expert_of == k, caps[k], limit)
    table = jnp.where(lane < limit, table, 0.0)
    high = table.astype(jnp.bfloat16).astype(jnp.float32)
    low = table - high

    mine = tok[...].astype(jnp.float32)[:CAP]
    top = jnp.concatenate([mine[:, :half], high], axis=1)
    bottom = jnp.concatenate([mine[:, half:], low], axis=1)
    own = slot(node, xi, core)
    gath[own] = jnp.concatenate([top, bottom], axis=0).astype(jnp.bfloat16)

    pl.semaphore_wait(barrier, len(peers))

    started = []
    pending = {}

    def send(key, index, s, peer):
        copy = remote(gath.at[s], gath.at[s], gs_sem.at[index], gr_sem.at[index], peer)
        copy.start()
        started.append(copy)
        pending[key] = copy

    for d in range(1, nodes):
        send(("z", d), d - 1, own, z_peer(d))
    send(("x", 0), nodes - 1, own, x_peer)
    send(("c", 0, 0), 2 * nodes - 1, own, core_peer)
    for d in range(1, nodes):
        pending[("z", d)].wait_recv()
        s = slot((node + nodes - d) % nodes, xi, core)
        send(("x", d), nodes - 1 + d, s, x_peer)
        send(("c", 0, d), 2 * nodes - 1 + d, s, core_peer)
    for d in range(nodes):
        pending[("x", d)].wait_recv()
        s = slot((node + nodes - d) % nodes, 1 - xi, core)
        send(("c", 1, d), 3 * nodes - 1 + d, s, core_peer)
    for x in range(2):
        for d in range(nodes):
            pending[("c", x, d)].wait_recv()

    got = gath[...].astype(jnp.float32)
    count = blocks * CAP
    rows[:, :half] = got[:, :CAP, :half].reshape(count, half).astype(jnp.bfloat16)
    rows[:, half:] = got[:, CAP:, :half].reshape(count, half).astype(jnp.bfloat16)
    expert = node * 2 + xi
    tables = got[:, :CAP, half:] + got[:, CAP:, half:]
    at_expert = lax.broadcasted_iota(jnp.int32, tables.shape, 1) == expert
    line = jnp.sum(jnp.where(at_expert, tables, 0.0), axis=1, keepdims=True)
    at_token = lax.broadcasted_iota(jnp.int32, tables.shape, 1) == lax.broadcasted_iota(jnp.int32, tables.shape, 2)
    weight = jnp.sum(jnp.where(at_token, line, 0.0), axis=2, keepdims=True).reshape(count, 1)

    loads[0].wait()
    loads[1].wait()
    step = 256
    for n in range(hidden // step):
        at = pl.ds(n * step, step)
        gated = jnp.dot(rows[...], wg[:, at], preferred_element_type=jnp.float32)
        upper = jnp.dot(rows[...], wu[:, at], preferred_element_type=jnp.float32)
        act[:, at] = (jax.nn.silu(gated) * upper * weight).astype(jnp.bfloat16)
    loads[2].wait()

    def down(c, k):
        at = pl.ds(pl.multiple_of(c * half + k * cols, LANES), cols)
        return jnp.dot(act[...], wd[:, at], preferred_element_type=jnp.float32)

    pair_copies, x_copies, z_copies = [], [], []
    for k in range(CHUNKS):
        pair_out[k] = down(1 - core, k).astype(jnp.bfloat16)
        copy = remote(pair_out.at[k], pair_in.at[k], ps_sem.at[k], pr_sem.at[k], core_peer)
        copy.start()
        pair_copies.append(copy)
    for k in range(CHUNKS):
        part = down(core, k)
        pair_copies[k].wait_recv()
        part = part + pair_in[k].astype(jnp.float32)
        summed[k] = part.reshape(nodes, 2, SHARDS * CAP, cols)
        x_out[k] = summed[k, :, 1 - xi].astype(jnp.bfloat16)
        copy = remote(x_out.at[k], x_in.at[k], xs_sem.at[k], xr_sem.at[k], x_peer)
        copy.start()
        x_copies.append(copy)
    for k in range(CHUNKS):
        x_copies[k].wait_recv()
        part = summed[k, :, xi] + x_in[k].astype(jnp.float32)
        total[k] = part
        z_out[k] = part.astype(jnp.bfloat16)
        for d in range(1, nodes):
            i = k * (nodes - 1) + d - 1
            copy = remote(
                z_out.at[k, (node + d) % nodes], z_in.at[k, d - 1], zs_sem.at[i], zr_sem.at[i], z_peer(d)
            )
            copy.start()
            z_copies.append(copy)
    fin_copies = []
    for k in range(CHUNKS):
        part = total[k, node]
        for d in range(1, nodes):
            z_copies[k * (nodes - 1) + d - 1].wait_recv()
            part = part + z_in[k, d - 1].astype(jnp.float32)
        fin[k, 0] = part[:CAP]
        fin[k, 1] = part[CAP:]
        copy = remote(fin.at[k, 1 - core], fin_in.at[k], fs_sem.at[k], fr_sem.at[k], core_peer)
        copy.start()
        fin_copies.append(copy)
    for k in range(CHUNKS):
        at = pl.ds(pl.multiple_of(core * half + k * cols, LANES), cols)
        out_ref[:, at] = fin[k, core]
    for k in range(CHUNKS):
        fin_copies[k].wait_recv()
        at = pl.ds(pl.multiple_of((1 - core) * half + k * cols, LANES), cols)
        out_ref[:, at] = fin_in[k]
    for copy in started + pair_copies + x_copies + z_copies + fin_copies:
        copy.wait_send()


def dense_device(tokens, routes, gates, capacity, w_gate, w_up, w_down):
    nodes = lax.axis_size("node")
    tok_count, width = tokens.shape
    hidden = w_gate.shape[2]
    half = width // 2
    cols = half // CHUNKS
    blocks = nodes * 2 * SHARDS
    count = blocks * CAP
    bf, f32 = jnp.bfloat16, jnp.float32
    vmem = pl.BlockSpec(memory_space=pltpu.VMEM)
    hbm = pl.BlockSpec(memory_space=pltpu.HBM)
    dma = pltpu.SemaphoreType.DMA
    pair_rows = SHARDS * CAP
    out = pl.pallas_call(
        functools.partial(dense_kernel, nodes),
        out_shape=jax.ShapeDtypeStruct((CAP, width), f32),
        in_specs=[hbm] * 7,
        out_specs=vmem,
        scratch_shapes=[
            pltpu.VMEM((width, hidden), bf),
            pltpu.VMEM((width, hidden), bf),
            pltpu.VMEM((hidden, width), bf),
            pltpu.VMEM((2 * CAP, width), bf),
            pltpu.VMEM(routes.shape[::-1], jnp.int32),
            pltpu.VMEM(gates.shape[::-1], f32),
            pltpu.SMEM(capacity.shape, jnp.int32),
            pltpu.VMEM((blocks, 2 * CAP, half + LANES), bf),
            pltpu.VMEM((count, width), bf),
            pltpu.VMEM((count, hidden), bf),
            pltpu.VMEM((CHUNKS, count, cols), bf),
            pltpu.VMEM((CHUNKS, count, cols), bf),
            pltpu.VMEM((CHUNKS, nodes, 2, pair_rows, cols), f32),
            pltpu.VMEM((CHUNKS, nodes, pair_rows, cols), bf),
            pltpu.VMEM((CHUNKS, nodes, pair_rows, cols), bf),
            pltpu.VMEM((CHUNKS, nodes, pair_rows, cols), f32),
            pltpu.VMEM((CHUNKS, nodes, pair_rows, cols), bf),
            pltpu.VMEM((CHUNKS, nodes - 1, pair_rows, cols), bf),
            pltpu.VMEM((CHUNKS, 2, CAP, cols), f32),
            pltpu.VMEM((CHUNKS, CAP, cols), f32),
            dma((7,)),
            dma((4 * nodes - 1,)),
            dma((4 * nodes - 1,)),
            dma((CHUNKS,)),
            dma((CHUNKS,)),
            dma((CHUNKS,)),
            dma((CHUNKS,)),
            dma((CHUNKS * (nodes - 1),)),
            dma((CHUNKS * (nodes - 1),)),
            dma((CHUNKS,)),
            dma((CHUNKS,)),
        ],
        compiler_params=pltpu.CompilerParams(
            collective_id=0, has_side_effects=True, vmem_limit_bytes=64 * 2**20
        ),
        cost_estimate=pl.CostEstimate(
            flops=6 * count * width * hidden, bytes_accessed=6 * width * hidden, transcendentals=count * hidden
        ),
    )(tokens, routes.T, gates.T, capacity, w_gate, w_up, w_down)
    return jnp.pad(out.astype(bf), ((0, tok_count - CAP), (0, 0)))


def per_device(tokens, routes, gates, capacity, w_gate, w_up, w_down):
    nodes = lax.axis_size("node")
    members = lax.axis_size("local")
    group_size = members // SHARDS
    experts = nodes * group_size
    tok_count, width = tokens.shape
    if experts == routes.shape[1] and group_size == 2 and members == 2 * SHARDS:
        return dense_device(tokens, routes, gates, capacity, w_gate, w_up, w_down)
    iota_e = jnp.arange(experts, dtype=jnp.int32)
    match = routes[:, :, None] == iota_e[None, None, :]
    chosen = jnp.sum(match.astype(jnp.int32), axis=1)
    gate_te = jnp.sum(jnp.where(match, gates[:, :, None], jnp.float32(0.0)), axis=1)
    rank = jnp.cumsum(chosen, axis=0) - chosen
    kept = (chosen > 0) & (rank < capacity[None, :])
    iota_c = jnp.arange(CAP, dtype=jnp.int32)
    place = (rank.T[:, None, :] == iota_c[None, :, None]) & kept.T[:, None, :]
    weighted = jnp.where(place, gate_te.T[:, None, :], jnp.float32(0.0))
    weighted = weighted.reshape(nodes, group_size, CAP, tok_count)
    gate_mat = w_gate[0]
    up_mat = w_up[0]
    down_mat = w_down[0]

    def read_back(back):
        back = back.reshape(nodes, group_size, SHARDS, CAP, width)
        return jnp.sum(back, axis=2).astype(jnp.bfloat16)

    place_bf = place.astype(jnp.bfloat16)
    slotted = jnp.einsum(
        "ect,td->ecd", place_bf, tokens, preferred_element_type=jnp.float32
    ).astype(jnp.bfloat16)
    slotted = slotted.reshape(nodes, group_size, CAP, width)
    wide = jnp.broadcast_to(slotted[:, :, None], (nodes, group_size, SHARDS, CAP, width))
    spread = wide.reshape(nodes, members, CAP, width)
    outgoing = spread.reshape(nodes * members, -1, width)
    arrived = lax.all_to_all(outgoing, ("node", "local"), split_axis=0, concat_axis=0, tiled=True)
    rows = arrived.reshape(-1, width)
    gated = jnp.dot(rows, gate_mat, preferred_element_type=jnp.float32)
    upper = jnp.dot(rows, up_mat, preferred_element_type=jnp.float32)
    act = (jax.nn.silu(gated) * upper).astype(jnp.bfloat16)
    back = lax.all_to_all(
        jnp.dot(act, down_mat, preferred_element_type=jnp.float32).reshape(arrived.shape),
        ("node", "local"),
        split_axis=0,
        concat_axis=0,
        tiled=True,
    )
    slot_gate = jnp.sum(weighted, axis=3)
    scaled = read_back(back).astype(jnp.float32) * slot_gate[:, :, :, None]
    high = scaled.astype(jnp.bfloat16)
    low = (scaled - high.astype(jnp.float32)).astype(jnp.bfloat16)
    pick = (weighted > 0.0).astype(jnp.bfloat16)
    summed = jnp.einsum("nmct,nmcd->ntd", pick, high, preferred_element_type=jnp.float32)
    summed = summed + jnp.einsum("nmct,nmcd->ntd", pick, low, preferred_element_type=jnp.float32)
    parts = summed.astype(jnp.bfloat16)
    return jnp.sum(parts.astype(jnp.float32), axis=0).astype(jnp.bfloat16)


def solution(mesh):
    return jax.shard_map(
        per_device,
        mesh=mesh,
        in_specs=(
            P(("replica", "node", "local"), None),
            P(("replica", "node", "local"), None),
            P(("replica", "node", "local"), None),
            P("replica"),
            P(("node", "local"), None, None),
            P(("node", "local"), None, None),
            P(("node", "local"), None, None),
        ),
        out_specs=P(("replica", "node", "local"), None),
        check_vma=False,
    )
```

```python
import functools

import jax
import jax.numpy as jnp
from jax import lax
from jax.experimental import pallas as pl
from jax.experimental.pallas import tpu as pltpu
from jax.sharding import PartitionSpec as P

SHARDS = 2
CAP = 8
LANES = 128
GROUPS = 4
MESH = pl.DeviceIdType.MESH


def dense_kernel(
    nodes,
    tokens_hbm, routes_hbm, gates_hbm, cap_hbm, wg_hbm, wu_hbm, wd_hbm,
    out_ref,
    wg, wu, wd, tok, routes_t, gates_t, caps, gath, rows, act,
    part_all, pair_out, pair_in, summed, x_out, x_in, z_out, z_in, fin,
    load_sem, gs_sem, gr_sem, ps_sem, pr_sem, xs_sem, xr_sem, zs_sem, zr_sem,
):
    node = lax.axis_index("node")
    local = lax.axis_index("local")
    xi = local // SHARDS
    core = local % SHARDS
    width = wg.shape[0]
    half = width // 2
    hidden = wg.shape[1]
    quarter = half // 2
    blocks = nodes * 2 * SHARDS

    core_peer = {"local": xi * SHARDS + 1 - core}
    x_peer = {"local": (1 - xi) * SHARDS + core}

    def z_peer(d):
        return {"node": (node + d) % nodes}

    def z_core_peer(d, c):
        return {"node": (node + d) % nodes, "local": xi * SHARDS + c}

    def slot(n, x, c):
        return (n * 2 + x) * SHARDS + c

    def remote(src, dst, send, recv, peer):
        return pltpu.make_async_remote_copy(
            src_ref=src, dst_ref=dst, send_sem=send, recv_sem=recv,
            device_id=peer, device_id_type=MESH,
        )

    barrier = pltpu.get_barrier_semaphore()
    peers = [core_peer, x_peer]
    peers += [z_core_peer(d, c) for d in range(1, nodes) for c in range(SHARDS)]
    for peer in peers:
        pl.semaphore_signal(barrier, inc=1, device_id=peer, device_id_type=MESH)

    small = [
        pltpu.make_async_copy(tokens_hbm.at[pl.ds(0, 2 * CAP)], tok, load_sem.at[0]),
        pltpu.make_async_copy(routes_hbm, routes_t, load_sem.at[4]),
        pltpu.make_async_copy(gates_hbm, gates_t, load_sem.at[5]),
        pltpu.make_async_copy(cap_hbm, caps, load_sem.at[6]),
    ]
    for load in small:
        load.start()
    loads = [
        pltpu.make_async_copy(wg_hbm.at[0], wg, load_sem.at[1]),
        pltpu.make_async_copy(wu_hbm.at[0], wu, load_sem.at[2]),
        pltpu.make_async_copy(wd_hbm.at[0], wd, load_sem.at[3]),
    ]
    for load in loads:
        load.start()

    for load in small:
        load.wait()
    lane = lax.broadcasted_iota(jnp.int32, (CAP, LANES), 1)
    expert_of = lax.broadcasted_iota(jnp.int32, (CAP, LANES), 0)
    pad = jnp.zeros((routes_t.shape[0], LANES - routes_t.shape[1]))
    ids = jnp.concatenate([routes_t[...], pad.astype(jnp.int32)], axis=1)
    gate = jnp.concatenate([gates_t[...], pad.astype(jnp.float32)], axis=1)
    table = jnp.zeros((CAP, LANES), jnp.float32)
    limit = jnp.zeros((CAP, LANES), jnp.int32)
    for k in range(routes_t.shape[0]):
        table = table + jnp.where(ids[k : k + 1] == expert_of, gate[k : k + 1], 0.0)
        limit = jnp.where(expert_of == k, caps[k], limit)
    table = jnp.where(lane < limit, table, 0.0)
    high = table.astype(jnp.bfloat16).astype(jnp.float32)
    low = table - high

    mine = tok[...].astype(jnp.float32)[:CAP]
    top = jnp.concatenate([mine[:, :half], high], axis=1)
    bottom = jnp.concatenate([mine[:, half:], low], axis=1)
    own = slot(node, xi, core)
    gath[own] = jnp.concatenate([top, bottom], axis=0).astype(jnp.bfloat16)

    pl.semaphore_wait(barrier, len(peers))

    started = []
    pending = {}

    def send(key, index, s, peer):
        copy = remote(gath.at[s], gath.at[s], gs_sem.at[index], gr_sem.at[index], peer)
        copy.start()
        started.append(copy)
        pending[key] = copy

    for d in range(1, nodes):
        send(("z", d), d - 1, own, z_peer(d))
    send(("x", 0), nodes - 1, own, x_peer)
    send(("c", 0, 0), 2 * nodes - 1, own, core_peer)
    for d in range(1, nodes):
        pending[("z", d)].wait_recv()
        s = slot((node + nodes - d) % nodes, xi, core)
        send(("x", d), nodes - 1 + d, s, x_peer)
        send(("c", 0, d), 2 * nodes - 1 + d, s, core_peer)
    for d in range(nodes):
        pending[("x", d)].wait_recv()
        s = slot((node + nodes - d) % nodes, 1 - xi, core)
        send(("c", 1, d), 3 * nodes - 1 + d, s, core_peer)
    for x in range(2):
        for d in range(nodes):
            pending[("c", x, d)].wait_recv()

    got = gath[...].astype(jnp.float32)
    count = blocks * CAP
    rows[:, :half] = got[:, :CAP, :half].reshape(count, half).astype(jnp.bfloat16)
    rows[:, half:] = got[:, CAP:, :half].reshape(count, half).astype(jnp.bfloat16)
    expert = node * 2 + xi
    tables = got[:, :CAP, half:] + got[:, CAP:, half:]
    at_expert = lax.broadcasted_iota(jnp.int32, tables.shape, 1) == expert
    line = jnp.sum(jnp.where(at_expert, tables, 0.0), axis=1, keepdims=True)
    at_token = lax.broadcasted_iota(jnp.int32, tables.shape, 1) == lax.broadcasted_iota(jnp.int32, tables.shape, 2)
    weight = jnp.sum(jnp.where(at_token, line, 0.0), axis=2, keepdims=True).reshape(count, 1)

    loads[0].wait()
    loads[1].wait()
    step = 256
    for n in range(hidden // step):
        at = pl.ds(n * step, step)
        gated = jnp.dot(rows[...], wg[:, at], preferred_element_type=jnp.float32)
        upper = jnp.dot(rows[...], wu[:, at], preferred_element_type=jnp.float32)
        act[:, at] = (jax.nn.silu(gated) * upper * weight).astype(jnp.bfloat16)
    loads[2].wait()

    def down(c):
        at = pl.ds(pl.multiple_of(c * half, LANES), half)
        part = jnp.dot(act[...], wd[:, at], preferred_element_type=jnp.float32)
        part_all[...] = part.reshape(part_all.shape)

    order = sorted(range(1, nodes), key=lambda d: -min(d, nodes - d)) + [0]
    size = nodes // GROUPS
    pair_copies, x_copies, z_copies = [], [], []
    down(1 - core)
    for g in range(GROUPS):
        for j in range(g * size, (g + 1) * size):
            pair_out[j] = part_all[(node + order[j]) % nodes].astype(jnp.bfloat16)
        at = pl.ds(g * size, size)
        copy = remote(pair_out.at[at], pair_in.at[at], ps_sem.at[g], pr_sem.at[g], core_peer)
        copy.start()
        pair_copies.append(copy)
    down(core)
    for g in range(GROUPS):
        pair_copies[g].wait_recv()
        for j in range(g * size, (g + 1) * size):
            summed[j] = part_all[(node + order[j]) % nodes] + pair_in[j].astype(jnp.float32)
            x_out[j] = summed[j, 1 - xi].astype(jnp.bfloat16)
        at = pl.ds(g * size, size)
        copy = remote(x_out.at[at], x_in.at[at], xs_sem.at[g], xr_sem.at[g], x_peer)
        copy.start()
        x_copies.append(copy)
    for j in range(nodes):
        if j % size == 0:
            x_copies[j // size].wait_recv()
        part = summed[j, xi] + x_in[j].astype(jnp.float32)
        for c in range(SHARDS):
            own_rows = part[c * CAP : (c + 1) * CAP]
            own_rows = jnp.concatenate([own_rows[:, :quarter], own_rows[:, quarter:]], axis=0)
            z_out[j, c] = own_rows.astype(jnp.bfloat16)
            if order[j]:
                copy = remote(
                    z_out.at[j, c], z_in.at[j, core], zs_sem.at[j, c], zr_sem.at[j, core], z_core_peer(order[j], c)
                )
                copy.start()
                z_copies.append(copy)
            else:
                fin[c] = own_rows
    last = nodes - 1
    copy = remote(
        z_out.at[last, 1 - core], z_in.at[last, core], zs_sem.at[last, 0], zr_sem.at[last, core], core_peer
    )
    copy.start()
    z_copies.append(copy)

    def arrival(j, c):
        return remote(z_out.at[j, 0], z_in.at[j, c], zs_sem.at[j, 0], zr_sem.at[j, c], core_peer)

    def put(c, value):
        for q in range(2):
            at = pl.ds(pl.multiple_of(c * half + q * quarter, LANES), quarter)
            rows_of = value[q * CAP : (q + 1) * CAP]
            out_ref[:, at] = jnp.concatenate([rows_of, jnp.zeros_like(rows_of)], axis=0).astype(jnp.bfloat16)

    mine = fin[core]
    arrival(last, 1 - core).wait_recv()
    other = z_in[last, 1 - core].astype(jnp.float32)
    for j in reversed(range(last)):
        arrival(j, core).wait_recv()
        mine = mine + z_in[j, core].astype(jnp.float32)
        arrival(j, 1 - core).wait_recv()
        other = other + z_in[j, 1 - core].astype(jnp.float32)
    put(core, mine)
    put(1 - core, other)
    for copy in started + pair_copies + x_copies + z_copies:
        copy.wait_send()


def dense_device(tokens, routes, gates, capacity, w_gate, w_up, w_down):
    nodes = lax.axis_size("node")
    tok_count, width = tokens.shape
    hidden = w_gate.shape[2]
    half = width // 2
    blocks = nodes * 2 * SHARDS
    count = blocks * CAP
    bf, f32 = jnp.bfloat16, jnp.float32
    vmem = pl.BlockSpec(memory_space=pltpu.VMEM)
    hbm = pl.BlockSpec(memory_space=pltpu.HBM)
    dma = pltpu.SemaphoreType.DMA
    pair_rows = SHARDS * CAP
    out = pl.pallas_call(
        functools.partial(dense_kernel, nodes),
        out_shape=jax.ShapeDtypeStruct((2 * CAP, width), bf),
        in_specs=[hbm] * 7,
        out_specs=vmem,
        scratch_shapes=[
            pltpu.VMEM((width, hidden), bf),
            pltpu.VMEM((width, hidden), bf),
            pltpu.VMEM((hidden, width), bf),
            pltpu.VMEM((2 * CAP, width), bf),
            pltpu.VMEM(routes.shape[::-1], jnp.int32),
            pltpu.VMEM(gates.shape[::-1], f32),
            pltpu.SMEM(capacity.shape, jnp.int32),
            pltpu.VMEM((blocks, 2 * CAP, half + LANES), bf),
            pltpu.VMEM((count, width), bf),
            pltpu.VMEM((count, hidden), bf),
            pltpu.VMEM((nodes, 2, pair_rows, half), f32),
            pltpu.VMEM((nodes, 2, pair_rows, half), bf),
            pltpu.VMEM((nodes, 2, pair_rows, half), bf),
            pltpu.VMEM((nodes, 2, pair_rows, half), f32),
            pltpu.VMEM((nodes, pair_rows, half), bf),
            pltpu.VMEM((nodes, pair_rows, half), bf),
            pltpu.VMEM((nodes, SHARDS, 2 * CAP, half // 2), bf),
            pltpu.VMEM((nodes, SHARDS, 2 * CAP, half // 2), bf),
            pltpu.VMEM((SHARDS, 2 * CAP, half // 2), f32),
            dma((7,)),
            dma((4 * nodes - 1,)),
            dma((4 * nodes - 1,)),
            dma((GROUPS,)),
            dma((GROUPS,)),
            dma((GROUPS,)),
            dma((GROUPS,)),
            dma((nodes, SHARDS)),
            dma((nodes, SHARDS)),
        ],
        compiler_params=pltpu.CompilerParams(
            collective_id=0, has_side_effects=True, vmem_limit_bytes=64 * 2**20
        ),
        cost_estimate=pl.CostEstimate(
            flops=6 * count * width * hidden, bytes_accessed=6 * width * hidden, transcendentals=count * hidden
        ),
    )(tokens, routes.T, gates.T, capacity, w_gate, w_up, w_down)
    return jnp.pad(out, ((0, tok_count - 2 * CAP), (0, 0)))


def per_device(tokens, routes, gates, capacity, w_gate, w_up, w_down):
    nodes = lax.axis_size("node")
    members = lax.axis_size("local")
    group_size = members // SHARDS
    experts = nodes * group_size
    tok_count, width = tokens.shape
    if experts == routes.shape[1] and group_size == 2 and members == 2 * SHARDS:
        return dense_device(tokens, routes, gates, capacity, w_gate, w_up, w_down)
    iota_e = jnp.arange(experts, dtype=jnp.int32)
    match = routes[:, :, None] == iota_e[None, None, :]
    chosen = jnp.sum(match.astype(jnp.int32), axis=1)
    gate_te = jnp.sum(jnp.where(match, gates[:, :, None], jnp.float32(0.0)), axis=1)
    rank = jnp.cumsum(chosen, axis=0) - chosen
    kept = (chosen > 0) & (rank < capacity[None, :])
    iota_c = jnp.arange(CAP, dtype=jnp.int32)
    place = (rank.T[:, None, :] == iota_c[None, :, None]) & kept.T[:, None, :]
    weighted = jnp.where(place, gate_te.T[:, None, :], jnp.float32(0.0))
    weighted = weighted.reshape(nodes, group_size, CAP, tok_count)
    gate_mat = w_gate[0]
    up_mat = w_up[0]
    down_mat = w_down[0]

    def read_back(back):
        back = back.reshape(nodes, group_size, SHARDS, CAP, width)
        return jnp.sum(back, axis=2).astype(jnp.bfloat16)

    place_bf = place.astype(jnp.bfloat16)
    slotted = jnp.einsum(
        "ect,td->ecd", place_bf, tokens, preferred_element_type=jnp.float32
    ).astype(jnp.bfloat16)
    slotted = slotted.reshape(nodes, group_size, CAP, width)
    wide = jnp.broadcast_to(slotted[:, :, None], (nodes, group_size, SHARDS, CAP, width))
    spread = wide.reshape(nodes, members, CAP, width)
    outgoing = spread.reshape(nodes * members, -1, width)
    arrived = lax.all_to_all(outgoing, ("node", "local"), split_axis=0, concat_axis=0, tiled=True)
    rows = arrived.reshape(-1, width)
    gated = jnp.dot(rows, gate_mat, preferred_element_type=jnp.float32)
    upper = jnp.dot(rows, up_mat, preferred_element_type=jnp.float32)
    act = (jax.nn.silu(gated) * upper).astype(jnp.bfloat16)
    back = lax.all_to_all(
        jnp.dot(act, down_mat, preferred_element_type=jnp.float32).reshape(arrived.shape),
        ("node", "local"),
        split_axis=0,
        concat_axis=0,
        tiled=True,
    )
    slot_gate = jnp.sum(weighted, axis=3)
    scaled = read_back(back).astype(jnp.float32) * slot_gate[:, :, :, None]
    high = scaled.astype(jnp.bfloat16)
    low = (scaled - high.astype(jnp.float32)).astype(jnp.bfloat16)
    pick = (weighted > 0.0).astype(jnp.bfloat16)
    summed = jnp.einsum("nmct,nmcd->ntd", pick, high, preferred_element_type=jnp.float32)
    summed = summed + jnp.einsum("nmct,nmcd->ntd", pick, low, preferred_element_type=jnp.float32)
    parts = summed.astype(jnp.bfloat16)
    return jnp.sum(parts.astype(jnp.float32), axis=0).astype(jnp.bfloat16)


def solution(mesh):
    return jax.shard_map(
        per_device,
        mesh=mesh,
        in_specs=(
            P(("replica", "node", "local"), None),
            P(("replica", "node", "local"), None),
            P(("replica", "node", "local"), None),
            P("replica"),
            P(("node", "local"), None, None),
            P(("node", "local"), None, None),
            P(("node", "local"), None, None),
        ),
        out_specs=P(("replica", "node", "local"), None),
        check_vma=False,
    )
```

```python
import functools

import jax
import jax.numpy as jnp
from jax import lax
from jax.experimental import pallas as pl
from jax.experimental.pallas import tpu as pltpu
from jax.sharding import PartitionSpec as P

SHARDS = 2
CAP = 8
LANES = 128
GROUPS = 4
MESH = pl.DeviceIdType.MESH


def dense_kernel(
    nodes,
    tokens_hbm, routes_hbm, gates_hbm, cap_hbm, wg_hbm, wu_hbm, wd_hbm,
    out_ref,
    wg, wu, wd, tok, routes_t, gates_t, caps, gath, rows, act,
    part_all, pair_out, pair_in, summed, x_out, x_in, z_out, z_in, fin,
    load_sem, gs_sem, gr_sem, ps_sem, pr_sem, xs_sem, xr_sem, zs_sem, zr_sem,
):
    node = lax.axis_index("node")
    local = lax.axis_index("local")
    xi = local // SHARDS
    core = local % SHARDS
    width = wg.shape[0]
    half = width // 2
    hidden = wg.shape[1]
    quarter = half // 2
    blocks = nodes * 2 * SHARDS

    core_peer = {"local": xi * SHARDS + 1 - core}
    x_peer = {"local": (1 - xi) * SHARDS + core}

    def z_peer(d):
        return {"node": (node + d) % nodes}

    def z_core_peer(d, c):
        return {"node": (node + d) % nodes, "local": xi * SHARDS + c}

    def slot(n, x, c):
        return (n * 2 + x) * SHARDS + c

    def remote(src, dst, send, recv, peer):
        return pltpu.make_async_remote_copy(
            src_ref=src, dst_ref=dst, send_sem=send, recv_sem=recv,
            device_id=peer, device_id_type=MESH,
        )

    small = [
        pltpu.make_async_copy(tokens_hbm.at[pl.ds(0, 2 * CAP)], tok, load_sem.at[0]),
        pltpu.make_async_copy(routes_hbm, routes_t, load_sem.at[4]),
        pltpu.make_async_copy(gates_hbm, gates_t, load_sem.at[5]),
        pltpu.make_async_copy(cap_hbm, caps, load_sem.at[6]),
    ]
    for load in small:
        load.start()
    barrier = pltpu.get_barrier_semaphore()
    peers = [core_peer, x_peer]
    peers += [z_core_peer(d, c) for d in range(1, nodes) for c in range(SHARDS)]
    for peer in peers:
        pl.semaphore_signal(barrier, inc=1, device_id=peer, device_id_type=MESH)

    loads = [
        pltpu.make_async_copy(wg_hbm.at[0], wg, load_sem.at[1]),
        pltpu.make_async_copy(wu_hbm.at[0], wu, load_sem.at[2]),
        pltpu.make_async_copy(wd_hbm.at[0], wd, load_sem.at[3]),
    ]

    for load in small:
        load.wait()
    lane = lax.broadcasted_iota(jnp.int32, (CAP, LANES), 1)
    expert_of = lax.broadcasted_iota(jnp.int32, (CAP, LANES), 0)
    pad = jnp.zeros((routes_t.shape[0], LANES - routes_t.shape[1]))
    ids = jnp.concatenate([routes_t[...], pad.astype(jnp.int32)], axis=1)
    gate = jnp.concatenate([gates_t[...], pad.astype(jnp.float32)], axis=1)
    table = jnp.zeros((CAP, LANES), jnp.float32)
    limit = jnp.zeros((CAP, LANES), jnp.int32)
    for k in range(routes_t.shape[0]):
        table = table + jnp.where(ids[k : k + 1] == expert_of, gate[k : k + 1], 0.0)
        limit = jnp.where(expert_of == k, caps[k], limit)
    table = jnp.where(lane < limit, table, 0.0)
    high = table.astype(jnp.bfloat16).astype(jnp.float32)
    low = table - high

    mine = tok[...].astype(jnp.float32)[:CAP]
    top = jnp.concatenate([mine[:, :half], high], axis=1)
    bottom = jnp.concatenate([mine[:, half:], low], axis=1)
    own = slot(node, xi, core)
    gath[own] = jnp.concatenate([top, bottom], axis=0).astype(jnp.bfloat16)

    pl.semaphore_wait(barrier, len(peers))

    started = []
    pending = {}

    def send(key, index, s, peer):
        copy = remote(gath.at[s], gath.at[s], gs_sem.at[index], gr_sem.at[index], peer)
        copy.start()
        started.append(copy)
        pending[key] = copy

    far = sorted(range(1, nodes), key=lambda d: -min(d, nodes - d))
    for d in far:
        send(("z", d), d - 1, own, z_peer(d))
    send(("x", 0), nodes - 1, own, x_peer)
    send(("c", 0, 0), 2 * nodes - 1, own, core_peer)
    for load in loads:
        load.start()
    for d in far:
        pending[("z", d)].wait_recv()
        s = slot((node + nodes - d) % nodes, xi, core)
        send(("x", d), nodes - 1 + d, s, x_peer)
        send(("c", 0, d), 2 * nodes - 1 + d, s, core_peer)
    for d in [0] + far:
        pending[("x", d)].wait_recv()
        s = slot((node + nodes - d) % nodes, 1 - xi, core)
        send(("c", 1, d), 3 * nodes - 1 + d, s, core_peer)
    for x in range(2):
        for d in range(nodes):
            pending[("c", x, d)].wait_recv()

    got = gath[...].astype(jnp.float32)
    count = blocks * CAP
    rows[:, :half] = got[:, :CAP, :half].reshape(count, half).astype(jnp.bfloat16)
    rows[:, half:] = got[:, CAP:, :half].reshape(count, half).astype(jnp.bfloat16)
    expert = node * 2 + xi
    tables = got[:, :CAP, half:] + got[:, CAP:, half:]
    at_expert = lax.broadcasted_iota(jnp.int32, tables.shape, 1) == expert
    line = jnp.sum(jnp.where(at_expert, tables, 0.0), axis=1, keepdims=True)
    at_token = lax.broadcasted_iota(jnp.int32, tables.shape, 1) == lax.broadcasted_iota(jnp.int32, tables.shape, 2)
    weight = jnp.sum(jnp.where(at_token, line, 0.0), axis=2, keepdims=True).reshape(count, 1)

    loads[0].wait()
    loads[1].wait()
    step = 256
    for n in range(hidden // step):
        at = pl.ds(n * step, step)
        gated = jnp.dot(rows[...], wg[:, at], preferred_element_type=jnp.float32)
        upper = jnp.dot(rows[...], wu[:, at], preferred_element_type=jnp.float32)
        act[:, at] = (jax.nn.silu(gated) * upper * weight).astype(jnp.bfloat16)
    loads[2].wait()

    def down(c):
        at = pl.ds(pl.multiple_of(c * half, LANES), half)
        part = jnp.dot(act[...], wd[:, at], preferred_element_type=jnp.float32)
        part_all[...] = part.reshape(part_all.shape)

    order = sorted(range(1, nodes), key=lambda d: -min(d, nodes - d)) + [0]
    size = nodes // GROUPS
    pair_copies, x_copies, z_copies = [], [], []
    down(1 - core)
    for g in range(GROUPS):
        for j in range(g * size, (g + 1) * size):
            pair_out[j] = part_all[(node + order[j]) % nodes].astype(jnp.bfloat16)
        at = pl.ds(g * size, size)
        copy = remote(pair_out.at[at], pair_in.at[at], ps_sem.at[g], pr_sem.at[g], core_peer)
        copy.start()
        pair_copies.append(copy)
    down(core)
    for g in range(GROUPS):
        pair_copies[g].wait_recv()
        for j in range(g * size, (g + 1) * size):
            summed[j] = part_all[(node + order[j]) % nodes] + pair_in[j].astype(jnp.float32)
            x_out[j] = summed[j, 1 - xi].astype(jnp.bfloat16)
        at = pl.ds(g * size, size)
        copy = remote(x_out.at[at], x_in.at[at], xs_sem.at[g], xr_sem.at[g], x_peer)
        copy.start()
        x_copies.append(copy)
    for j in range(nodes):
        if j % size == 0:
            x_copies[j // size].wait_recv()
        part = summed[j, xi] + x_in[j].astype(jnp.float32)
        for c in range(SHARDS):
            own_rows = part[c * CAP : (c + 1) * CAP]
            own_rows = jnp.concatenate([own_rows[:, :quarter], own_rows[:, quarter:]], axis=0)
            z_out[j, c] = own_rows.astype(jnp.bfloat16)
            if order[j]:
                copy = remote(
                    z_out.at[j, c], z_in.at[j, core], zs_sem.at[j, c], zr_sem.at[j, core], z_core_peer(order[j], c)
                )
                copy.start()
                z_copies.append(copy)
            else:
                fin[c] = own_rows
    last = nodes - 1
    copy = remote(
        z_out.at[last, 1 - core], z_in.at[last, core], zs_sem.at[last, 0], zr_sem.at[last, core], core_peer
    )
    copy.start()
    z_copies.append(copy)

    def arrival(j, c):
        return remote(z_out.at[j, 0], z_in.at[j, c], zs_sem.at[j, 0], zr_sem.at[j, c], core_peer)

    def put(c, value):
        for q in range(2):
            at = pl.ds(pl.multiple_of(c * half + q * quarter, LANES), quarter)
            rows_of = value[q * CAP : (q + 1) * CAP]
            out_ref[:, at] = jnp.concatenate([rows_of, jnp.zeros_like(rows_of)], axis=0).astype(jnp.bfloat16)

    mine = fin[core]
    arrival(last, 1 - core).wait_recv()
    other = z_in[last, 1 - core].astype(jnp.float32)
    for j in reversed(range(last)):
        arrival(j, core).wait_recv()
        mine = mine + z_in[j, core].astype(jnp.float32)
        arrival(j, 1 - core).wait_recv()
        other = other + z_in[j, 1 - core].astype(jnp.float32)
    put(core, mine)
    put(1 - core, other)
    for copy in started + pair_copies + x_copies + z_copies:
        copy.wait_send()


def dense_device(tokens, routes, gates, capacity, w_gate, w_up, w_down):
    nodes = lax.axis_size("node")
    tok_count, width = tokens.shape
    hidden = w_gate.shape[2]
    half = width // 2
    blocks = nodes * 2 * SHARDS
    count = blocks * CAP
    bf, f32 = jnp.bfloat16, jnp.float32
    vmem = pl.BlockSpec(memory_space=pltpu.VMEM)
    hbm = pl.BlockSpec(memory_space=pltpu.HBM)
    dma = pltpu.SemaphoreType.DMA
    pair_rows = SHARDS * CAP
    out = pl.pallas_call(
        functools.partial(dense_kernel, nodes),
        out_shape=jax.ShapeDtypeStruct((2 * CAP, width), bf),
        in_specs=[hbm] * 7,
        out_specs=vmem,
        scratch_shapes=[
            pltpu.VMEM((width, hidden), bf),
            pltpu.VMEM((width, hidden), bf),
            pltpu.VMEM((hidden, width), bf),
            pltpu.VMEM((2 * CAP, width), bf),
            pltpu.VMEM(routes.shape[::-1], jnp.int32),
            pltpu.VMEM(gates.shape[::-1], f32),
            pltpu.SMEM(capacity.shape, jnp.int32),
            pltpu.VMEM((blocks, 2 * CAP, half + LANES), bf),
            pltpu.VMEM((count, width), bf),
            pltpu.VMEM((count, hidden), bf),
            pltpu.VMEM((nodes, 2, pair_rows, half), f32),
            pltpu.VMEM((nodes, 2, pair_rows, half), bf),
            pltpu.VMEM((nodes, 2, pair_rows, half), bf),
            pltpu.VMEM((nodes, 2, pair_rows, half), f32),
            pltpu.VMEM((nodes, pair_rows, half), bf),
            pltpu.VMEM((nodes, pair_rows, half), bf),
            pltpu.VMEM((nodes, SHARDS, 2 * CAP, half // 2), bf),
            pltpu.VMEM((nodes, SHARDS, 2 * CAP, half // 2), bf),
            pltpu.VMEM((SHARDS, 2 * CAP, half // 2), f32),
            dma((7,)),
            dma((4 * nodes - 1,)),
            dma((4 * nodes - 1,)),
            dma((GROUPS,)),
            dma((GROUPS,)),
            dma((GROUPS,)),
            dma((GROUPS,)),
            dma((nodes, SHARDS)),
            dma((nodes, SHARDS)),
        ],
        compiler_params=pltpu.CompilerParams(
            collective_id=0, has_side_effects=True, vmem_limit_bytes=64 * 2**20
        ),
        cost_estimate=pl.CostEstimate(
            flops=6 * count * width * hidden, bytes_accessed=6 * width * hidden, transcendentals=count * hidden
        ),
    )(tokens, routes.T, gates.T, capacity, w_gate, w_up, w_down)
    return jnp.pad(out, ((0, tok_count - 2 * CAP), (0, 0)))


def per_device(tokens, routes, gates, capacity, w_gate, w_up, w_down):
    nodes = lax.axis_size("node")
    members = lax.axis_size("local")
    group_size = members // SHARDS
    experts = nodes * group_size
    tok_count, width = tokens.shape
    if experts == routes.shape[1] and group_size == 2 and members == 2 * SHARDS:
        return dense_device(tokens, routes, gates, capacity, w_gate, w_up, w_down)
    iota_e = jnp.arange(experts, dtype=jnp.int32)
    match = routes[:, :, None] == iota_e[None, None, :]
    chosen = jnp.sum(match.astype(jnp.int32), axis=1)
    gate_te = jnp.sum(jnp.where(match, gates[:, :, None], jnp.float32(0.0)), axis=1)
    rank = jnp.cumsum(chosen, axis=0) - chosen
    kept = (chosen > 0) & (rank < capacity[None, :])
    iota_c = jnp.arange(CAP, dtype=jnp.int32)
    place = (rank.T[:, None, :] == iota_c[None, :, None]) & kept.T[:, None, :]
    weighted = jnp.where(place, gate_te.T[:, None, :], jnp.float32(0.0))
    weighted = weighted.reshape(nodes, group_size, CAP, tok_count)
    gate_mat = w_gate[0]
    up_mat = w_up[0]
    down_mat = w_down[0]

    def read_back(back):
        back = back.reshape(nodes, group_size, SHARDS, CAP, width)
        return jnp.sum(back, axis=2).astype(jnp.bfloat16)

    place_bf = place.astype(jnp.bfloat16)
    slotted = jnp.einsum(
        "ect,td->ecd", place_bf, tokens, preferred_element_type=jnp.float32
    ).astype(jnp.bfloat16)
    slotted = slotted.reshape(nodes, group_size, CAP, width)
    wide = jnp.broadcast_to(slotted[:, :, None], (nodes, group_size, SHARDS, CAP, width))
    spread = wide.reshape(nodes, members, CAP, width)
    outgoing = spread.reshape(nodes * members, -1, width)
    arrived = lax.all_to_all(outgoing, ("node", "local"), split_axis=0, concat_axis=0, tiled=True)
    rows = arrived.reshape(-1, width)
    gated = jnp.dot(rows, gate_mat, preferred_element_type=jnp.float32)
    upper = jnp.dot(rows, up_mat, preferred_element_type=jnp.float32)
    act = (jax.nn.silu(gated) * upper).astype(jnp.bfloat16)
    back = lax.all_to_all(
        jnp.dot(act, down_mat, preferred_element_type=jnp.float32).reshape(arrived.shape),
        ("node", "local"),
        split_axis=0,
        concat_axis=0,
        tiled=True,
    )
    slot_gate = jnp.sum(weighted, axis=3)
    scaled = read_back(back).astype(jnp.float32) * slot_gate[:, :, :, None]
    high = scaled.astype(jnp.bfloat16)
    low = (scaled - high.astype(jnp.float32)).astype(jnp.bfloat16)
    pick = (weighted > 0.0).astype(jnp.bfloat16)
    summed = jnp.einsum("nmct,nmcd->ntd", pick, high, preferred_element_type=jnp.float32)
    summed = summed + jnp.einsum("nmct,nmcd->ntd", pick, low, preferred_element_type=jnp.float32)
    parts = summed.astype(jnp.bfloat16)
    return jnp.sum(parts.astype(jnp.float32), axis=0).astype(jnp.bfloat16)


def solution(mesh):
    return jax.shard_map(
        per_device,
        mesh=mesh,
        in_specs=(
            P(("replica", "node", "local"), None),
            P(("replica", "node", "local"), None),
            P(("replica", "node", "local"), None),
            P("replica"),
            P(("node", "local"), None, None),
            P(("node", "local"), None, None),
            P(("node", "local"), None, None),
        ),
        out_specs=P(("replica", "node", "local"), None),
        check_vma=False,
    )
```

```python
import functools

import jax
import jax.numpy as jnp
from jax import lax
from jax.experimental import pallas as pl
from jax.experimental.pallas import tpu as pltpu
from jax.sharding import PartitionSpec as P

SHARDS = 2
CAP = 8
LANES = 128
GROUPS = 4
MESH = pl.DeviceIdType.MESH


def dense_kernel(
    nodes,
    tokens_hbm, routes_hbm, gates_hbm, cap_hbm, wg_hbm, wu_hbm, wd_hbm,
    out_ref,
    wg, wu, wd, tok, routes_t, gates_t, caps, gath, rows, act,
    part_all, pair_out, pair_in, x_out, x_in, z_out, z_in, fin,
    load_sem, gs_sem, gr_sem, ps_sem, pr_sem, xs_sem, xr_sem, zs_sem, zr_sem,
):
    node = lax.axis_index("node")
    local = lax.axis_index("local")
    xi = local // SHARDS
    core = local % SHARDS
    width = wg.shape[0]
    half = width // 2
    hidden = wg.shape[1]
    quarter = half // 2
    blocks = nodes * 2 * SHARDS

    core_peer = {"local": xi * SHARDS + 1 - core}
    x_peer = {"local": (1 - xi) * SHARDS + core}

    def z_peer(d):
        return {"node": (node + d) % nodes}

    def z_core_peer(d, c):
        return {"node": (node + d) % nodes, "local": xi * SHARDS + c}

    def slot(n, x, c):
        return (n * 2 + x) * SHARDS + c

    def remote(src, dst, send, recv, peer):
        return pltpu.make_async_remote_copy(
            src_ref=src, dst_ref=dst, send_sem=send, recv_sem=recv,
            device_id=peer, device_id_type=MESH,
        )

    small = [
        pltpu.make_async_copy(tokens_hbm.at[pl.ds(0, 2 * CAP)], tok, load_sem.at[0]),
        pltpu.make_async_copy(routes_hbm, routes_t, load_sem.at[4]),
        pltpu.make_async_copy(gates_hbm, gates_t, load_sem.at[5]),
        pltpu.make_async_copy(cap_hbm, caps, load_sem.at[6]),
    ]
    for load in small:
        load.start()
    barrier = pltpu.get_barrier_semaphore()
    peers = [core_peer, x_peer]
    peers += [z_core_peer(d, c) for d in range(1, nodes) for c in range(SHARDS)]
    for peer in peers:
        pl.semaphore_signal(barrier, inc=1, device_id=peer, device_id_type=MESH)

    loads = [
        pltpu.make_async_copy(wg_hbm.at[0], wg, load_sem.at[1]),
        pltpu.make_async_copy(wu_hbm.at[0], wu, load_sem.at[2]),
        pltpu.make_async_copy(wd_hbm.at[0], wd, load_sem.at[3]),
    ]

    for load in small:
        load.wait()
    lane = lax.broadcasted_iota(jnp.int32, (CAP, LANES), 1)
    expert_of = lax.broadcasted_iota(jnp.int32, (CAP, LANES), 0)
    pad = jnp.zeros((routes_t.shape[0], LANES - routes_t.shape[1]))
    ids = jnp.concatenate([routes_t[...], pad.astype(jnp.int32)], axis=1)
    gate = jnp.concatenate([gates_t[...], pad.astype(jnp.float32)], axis=1)
    table = jnp.zeros((CAP, LANES), jnp.float32)
    limit = jnp.zeros((CAP, LANES), jnp.int32)
    for k in range(routes_t.shape[0]):
        table = table + jnp.where(ids[k : k + 1] == expert_of, gate[k : k + 1], 0.0)
        limit = jnp.where(expert_of == k, caps[k], limit)
    table = jnp.where(lane < limit, table, 0.0)
    high = table.astype(jnp.bfloat16).astype(jnp.float32)
    low = table - high

    mine = tok[...].astype(jnp.float32)[:CAP]
    top = jnp.concatenate([mine[:, :half], high], axis=1)
    bottom = jnp.concatenate([mine[:, half:], low], axis=1)
    own = slot(node, xi, core)
    gath[own] = jnp.concatenate([top, bottom], axis=0).astype(jnp.bfloat16)

    pl.semaphore_wait(barrier, len(peers))

    started = []
    pending = {}

    def send(key, index, s, peer):
        copy = remote(gath.at[s], gath.at[s], gs_sem.at[index], gr_sem.at[index], peer)
        copy.start()
        started.append(copy)
        pending[key] = copy

    far = sorted(range(1, nodes), key=lambda d: -min(d, nodes - d))
    for d in far:
        send(("z", d), d - 1, own, z_peer(d))
    send(("x", 0), nodes - 1, own, x_peer)
    send(("c", 0, 0), 2 * nodes - 1, own, core_peer)
    for load in loads:
        load.start()
    for d in far:
        pending[("z", d)].wait_recv()
        s = slot((node + nodes - d) % nodes, xi, core)
        send(("x", d), nodes - 1 + d, s, x_peer)
        send(("c", 0, d), 2 * nodes - 1 + d, s, core_peer)
    for d in [0] + far:
        pending[("x", d)].wait_recv()
        s = slot((node + nodes - d) % nodes, 1 - xi, core)
        send(("c", 1, d), 3 * nodes - 1 + d, s, core_peer)
    for x in range(2):
        for d in range(nodes):
            pending[("c", x, d)].wait_recv()

    got = gath[...].astype(jnp.float32)
    count = blocks * CAP
    rows[:, :half] = got[:, :CAP, :half].reshape(count, half).astype(jnp.bfloat16)
    rows[:, half:] = got[:, CAP:, :half].reshape(count, half).astype(jnp.bfloat16)
    expert = node * 2 + xi
    tables = got[:, :CAP, half:] + got[:, CAP:, half:]
    at_expert = lax.broadcasted_iota(jnp.int32, tables.shape, 1) == expert
    line = jnp.sum(jnp.where(at_expert, tables, 0.0), axis=1, keepdims=True)
    at_token = lax.broadcasted_iota(jnp.int32, tables.shape, 1) == lax.broadcasted_iota(jnp.int32, tables.shape, 2)
    weight = jnp.sum(jnp.where(at_token, line, 0.0), axis=2, keepdims=True).reshape(count, 1)

    loads[0].wait()
    loads[1].wait()
    step = 256
    for n in range(hidden // step):
        at = pl.ds(n * step, step)
        gated = jnp.dot(rows[...], wg[:, at], preferred_element_type=jnp.float32)
        upper = jnp.dot(rows[...], wu[:, at], preferred_element_type=jnp.float32)
        act[:, at] = (jax.nn.silu(gated) * upper * weight).astype(jnp.bfloat16)
    loads[2].wait()

    def down(c):
        at = pl.ds(pl.multiple_of(c * half, LANES), half)
        part = jnp.dot(act[...], wd[:, at], preferred_element_type=jnp.float32)
        part_all[...] = part.reshape(part_all.shape)

    order = sorted(range(1, nodes), key=lambda d: -min(d, nodes - d)) + [0]
    size = nodes // GROUPS
    pair_copies, x_copies, z_copies = [], [], []
    down(1 - core)
    for g in range(GROUPS):
        for j in range(g * size, (g + 1) * size):
            pair_out[j] = part_all[(node + order[j]) % nodes].astype(jnp.bfloat16)
        at = pl.ds(g * size, size)
        copy = remote(pair_out.at[at], pair_in.at[at], ps_sem.at[g], pr_sem.at[g], core_peer)
        copy.start()
        pair_copies.append(copy)
    down(core)
    for g in range(GROUPS):
        pair_copies[g].wait_recv()
        for j in range(g * size, (g + 1) * size):
            part = part_all[(node + order[j]) % nodes, 1 - xi] + pair_in[j, 1 - xi].astype(jnp.float32)
            x_out[j] = part.astype(jnp.bfloat16)
        at = pl.ds(g * size, size)
        copy = remote(x_out.at[at], x_in.at[at], xs_sem.at[g], xr_sem.at[g], x_peer)
        copy.start()
        x_copies.append(copy)
    for j in range(nodes):
        if j % size == 0:
            x_copies[j // size].wait_recv()
        part = part_all[(node + order[j]) % nodes, xi] + pair_in[j, xi].astype(jnp.float32)
        part = part + x_in[j].astype(jnp.float32)
        for c in range(SHARDS):
            own_rows = part[c * CAP : (c + 1) * CAP]
            own_rows = jnp.concatenate([own_rows[:, :quarter], own_rows[:, quarter:]], axis=0)
            z_out[j, c] = own_rows.astype(jnp.bfloat16)
            if order[j]:
                copy = remote(
                    z_out.at[j, c], z_in.at[j, core], zs_sem.at[j, c], zr_sem.at[j, core], z_core_peer(order[j], c)
                )
                copy.start()
                z_copies.append(copy)
            else:
                fin[c] = own_rows
    last = nodes - 1
    copy = remote(
        z_out.at[last, 1 - core], z_in.at[last, core], zs_sem.at[last, 0], zr_sem.at[last, core], core_peer
    )
    copy.start()
    z_copies.append(copy)

    def arrival(j, c):
        return remote(z_out.at[j, 0], z_in.at[j, c], zs_sem.at[j, 0], zr_sem.at[j, c], core_peer)

    def put(c, value):
        for q in range(2):
            at = pl.ds(pl.multiple_of(c * half + q * quarter, LANES), quarter)
            rows_of = value[q * CAP : (q + 1) * CAP]
            out_ref[:, at] = jnp.concatenate([rows_of, jnp.zeros_like(rows_of)], axis=0).astype(jnp.bfloat16)

    mine = fin[core]
    arrival(last, 1 - core).wait_recv()
    other = z_in[last, 1 - core].astype(jnp.float32)
    for j in reversed(range(last)):
        arrival(j, core).wait_recv()
        mine = mine + z_in[j, core].astype(jnp.float32)
        arrival(j, 1 - core).wait_recv()
        other = other + z_in[j, 1 - core].astype(jnp.float32)
    put(core, mine)
    put(1 - core, other)
    for copy in started + pair_copies + x_copies + z_copies:
        copy.wait_send()


def dense_device(tokens, routes, gates, capacity, w_gate, w_up, w_down):
    nodes = lax.axis_size("node")
    tok_count, width = tokens.shape
    hidden = w_gate.shape[2]
    half = width // 2
    blocks = nodes * 2 * SHARDS
    count = blocks * CAP
    bf, f32 = jnp.bfloat16, jnp.float32
    vmem = pl.BlockSpec(memory_space=pltpu.VMEM)
    hbm = pl.BlockSpec(memory_space=pltpu.HBM)
    dma = pltpu.SemaphoreType.DMA
    pair_rows = SHARDS * CAP
    out = pl.pallas_call(
        functools.partial(dense_kernel, nodes),
        out_shape=jax.ShapeDtypeStruct((2 * CAP, width), bf),
        in_specs=[hbm] * 7,
        out_specs=vmem,
        scratch_shapes=[
            pltpu.VMEM((width, hidden), bf),
            pltpu.VMEM((width, hidden), bf),
            pltpu.VMEM((hidden, width), bf),
            pltpu.VMEM((2 * CAP, width), bf),
            pltpu.VMEM(routes.shape[::-1], jnp.int32),
            pltpu.VMEM(gates.shape[::-1], f32),
            pltpu.SMEM(capacity.shape, jnp.int32),
            pltpu.VMEM((blocks, 2 * CAP, half + LANES), bf),
            pltpu.VMEM((count, width), bf),
            pltpu.VMEM((count, hidden), bf),
            pltpu.VMEM((nodes, 2, pair_rows, half), f32),
            pltpu.VMEM((nodes, 2, pair_rows, half), bf),
            pltpu.VMEM((nodes, 2, pair_rows, half), bf),
            pltpu.VMEM((nodes, pair_rows, half), bf),
            pltpu.VMEM((nodes, pair_rows, half), bf),
            pltpu.VMEM((nodes, SHARDS, 2 * CAP, half // 2), bf),
            pltpu.VMEM((nodes, SHARDS, 2 * CAP, half // 2), bf),
            pltpu.VMEM((SHARDS, 2 * CAP, half // 2), f32),
            dma((7,)),
            dma((4 * nodes - 1,)),
            dma((4 * nodes - 1,)),
            dma((GROUPS,)),
            dma((GROUPS,)),
            dma((GROUPS,)),
            dma((GROUPS,)),
            dma((nodes, SHARDS)),
            dma((nodes, SHARDS)),
        ],
        compiler_params=pltpu.CompilerParams(
            collective_id=0, has_side_effects=True, vmem_limit_bytes=64 * 2**20
        ),
        cost_estimate=pl.CostEstimate(
            flops=6 * count * width * hidden, bytes_accessed=6 * width * hidden, transcendentals=count * hidden
        ),
    )(tokens, routes.T, gates.T, capacity, w_gate, w_up, w_down)
    return jnp.pad(out, ((0, tok_count - 2 * CAP), (0, 0)))


def per_device(tokens, routes, gates, capacity, w_gate, w_up, w_down):
    nodes = lax.axis_size("node")
    members = lax.axis_size("local")
    group_size = members // SHARDS
    experts = nodes * group_size
    tok_count, width = tokens.shape
    if experts == routes.shape[1] and group_size == 2 and members == 2 * SHARDS:
        return dense_device(tokens, routes, gates, capacity, w_gate, w_up, w_down)
    iota_e = jnp.arange(experts, dtype=jnp.int32)
    match = routes[:, :, None] == iota_e[None, None, :]
    chosen = jnp.sum(match.astype(jnp.int32), axis=1)
    gate_te = jnp.sum(jnp.where(match, gates[:, :, None], jnp.float32(0.0)), axis=1)
    rank = jnp.cumsum(chosen, axis=0) - chosen
    kept = (chosen > 0) & (rank < capacity[None, :])
    iota_c = jnp.arange(CAP, dtype=jnp.int32)
    place = (rank.T[:, None, :] == iota_c[None, :, None]) & kept.T[:, None, :]
    weighted = jnp.where(place, gate_te.T[:, None, :], jnp.float32(0.0))
    weighted = weighted.reshape(nodes, group_size, CAP, tok_count)
    gate_mat = w_gate[0]
    up_mat = w_up[0]
    down_mat = w_down[0]

    def read_back(back):
        back = back.reshape(nodes, group_size, SHARDS, CAP, width)
        return jnp.sum(back, axis=2).astype(jnp.bfloat16)

    place_bf = place.astype(jnp.bfloat16)
    slotted = jnp.einsum(
        "ect,td->ecd", place_bf, tokens, preferred_element_type=jnp.float32
    ).astype(jnp.bfloat16)
    slotted = slotted.reshape(nodes, group_size, CAP, width)
    wide = jnp.broadcast_to(slotted[:, :, None], (nodes, group_size, SHARDS, CAP, width))
    spread = wide.reshape(nodes, members, CAP, width)
    outgoing = spread.reshape(nodes * members, -1, width)
    arrived = lax.all_to_all(outgoing, ("node", "local"), split_axis=0, concat_axis=0, tiled=True)
    rows = arrived.reshape(-1, width)
    gated = jnp.dot(rows, gate_mat, preferred_element_type=jnp.float32)
    upper = jnp.dot(rows, up_mat, preferred_element_type=jnp.float32)
    act = (jax.nn.silu(gated) * upper).astype(jnp.bfloat16)
    back = lax.all_to_all(
        jnp.dot(act, down_mat, preferred_element_type=jnp.float32).reshape(arrived.shape),
        ("node", "local"),
        split_axis=0,
        concat_axis=0,
        tiled=True,
    )
    slot_gate = jnp.sum(weighted, axis=3)
    scaled = read_back(back).astype(jnp.float32) * slot_gate[:, :, :, None]
    high = scaled.astype(jnp.bfloat16)
    low = (scaled - high.astype(jnp.float32)).astype(jnp.bfloat16)
    pick = (weighted > 0.0).astype(jnp.bfloat16)
    summed = jnp.einsum("nmct,nmcd->ntd", pick, high, preferred_element_type=jnp.float32)
    summed = summed + jnp.einsum("nmct,nmcd->ntd", pick, low, preferred_element_type=jnp.float32)
    parts = summed.astype(jnp.bfloat16)
    return jnp.sum(parts.astype(jnp.float32), axis=0).astype(jnp.bfloat16)


def solution(mesh):
    return jax.shard_map(
        per_device,
        mesh=mesh,
        in_specs=(
            P(("replica", "node", "local"), None),
            P(("replica", "node", "local"), None),
            P(("replica", "node", "local"), None),
            P("replica"),
            P(("node", "local"), None, None),
            P(("node", "local"), None, None),
            P(("node", "local"), None, None),
        ),
        out_specs=P(("replica", "node", "local"), None),
        check_vma=False,
    )
```
